32 devices in a mesh: groups: 2 (over y), wide: 4 (over x, core), narrow: 4 (over z).
Axes of the slice: x: 2, y: 2, z: 4, core: 2. Of those that a mesh axis runs over, the one named last changes fastest.
Arguments:
- centers: bfloat16 [8192, 1280], P(('groups', 'wide')), parts along dimension 0, may hold values from -6 to 6
- coefs: float32 [8192, 1000], P(('groups', 'wide', 'narrow')), parts along dimension 0, may hold values from -6 to 6
- slots: int32 [8, 1024], P(('groups', 'wide')), parts along dimension 0, may hold values from 0 to 1023, each once within a row
- pool: bfloat16 [8, 1024, 1280], P(('groups', 'narrow')), parts along dimension 0, may hold values from -6 to 6
- labels: bfloat16 [8, 1024, 1000], P(('groups', 'narrow')), parts along dimension 0, may hold values from -6 to 6
- order: int32 [8, 1024], P(('groups', 'narrow')), parts along dimension 0, may hold values from 0 to 1023, each once within a row
Outputs:
- new_coefs: float32 [8192, 1000], P(('groups', 'wide', 'narrow')), parts along dimension 0
- last_residual: bfloat16 [8, 512, 1000], P(('groups', 'narrow'), 'wide'), parts along dimension 0
The draws below stay inside these ranges and needn't reach their ends.
There are 2 independent parts, one for each index of `groups`. The reference program is written for one: setup_inputs(seed, part) draws one part's arguments, and reference() takes and returns one part's arrays. A program takes and returns all parts, laid end to end along the dimension named above; each array names one. Nothing has to cross between parts.
Inputs may be any that keep to these rules, and one draw needn't show every extreme that they name: Each row of slots is a permutation of the slots of one shard. Each row of order names every sample of its member once.
All inputs are finite; a program needn't handle non-finite values.
Results may differ from the reference program's by a relative error of at most 0.008.
Values may be sent and summed in bfloat16 or wider, within the bound.
A program may use at most 64 MiB of HBM per device.

```python
import math
import jax
import jax.numpy as jnp
from jax import lax

D = 1280
C = 1000
CEN_DEV = 1024
B = 512
INNER = 2
POOL = 1024
SHARDS = 4
MEMBERS = 4
CENTERS = 4096


def level_of(own_key, dims, pieces, low, top_value):
    def one(dim, blocks):
        draws = jax.random.uniform(jax.random.fold_in(jax.random.fold_in(own_key, 6), dim), (blocks,), jnp.float32, low / len(pieces), top_value / len(pieces))
        return jnp.repeat(jnp.exp(draws), dims[dim] // blocks).reshape((-1,) + (1,) * (len(dims) - dim - 1))

    loudness = one(*pieces[0])
    for cut in pieces[1:]:
        loudness = loudness * one(*cut)
    return loudness


def centred(own_key, extent, deviation, bound, cuts=(), dtype=jnp.bfloat16):
    factor_of = level_of(own_key, extent, cuts, -0.22, 0.18) if cuts else 1.0
    values = jax.random.normal(own_key, extent, jnp.float32) * deviation * factor_of
    return jnp.minimum(jnp.maximum(values, -bound), bound).astype(dtype)


def setup_inputs(seed: int = 0, part: int = 0) -> dict:
    keys = jax.random.split(jax.random.key(seed), 7)
    own_keys = jax.random.split(jax.random.fold_in(keys[6], part), 7)
    centers = centred(own_keys[0], (CENTERS, D), 1.0, 6.0, ((0, 4),))
    coefs = centred(own_keys[1], (CENTERS, C), 1.0, 6.0, ((0, 16),), jnp.float32)
    slots = jax.vmap(lambda own: jax.random.permutation(own, CEN_DEV))(jax.random.split(own_keys[2], SHARDS)).reshape((SHARDS, CEN_DEV)).astype(jnp.int32)
    pool = centred(own_keys[3], (MEMBERS, POOL, D), 1.0, 6.0, ((0, 4),))
    labels = centred(own_keys[4], (MEMBERS, POOL, C), 1.0, 6.0, ((0, 4),))
    order = jax.vmap(lambda own: jax.random.permutation(own, POOL))(jax.random.split(own_keys[5], MEMBERS)).reshape((MEMBERS, POOL)).astype(jnp.int32)
    return {"centers": centers, "coefs": coefs, "slots": slots, "pool": pool, "labels": labels, "order": order}


def unit_rows(values):
    widened = values.astype(jnp.float32)
    scale = lax.rsqrt(lax.optimization_barrier(jnp.sum(widened * widened, axis=-1, keepdims=True)) + 1e-06)
    return (widened * scale).astype(jnp.bfloat16)

def kernel_block(left, right, sharpness):
    cosine = lax.dot_general(left, right, (((1,), (1,)), ((), ())), preferred_element_type=jnp.float32)
    distance = jnp.sqrt(2.0 - 2.0 * cosine + 0.01)
    return jnp.exp((math.sqrt(2.01) - distance) * sharpness).astype(jnp.bfloat16)

def reference(centers, coefs, slots, pool, labels, order):
    sharpness = math.sqrt(D) / 1.5
    inv_root = 1.0 / math.sqrt(CENTERS)
    shards = centers.reshape(SHARDS, CEN_DEV, D)
    placed = jnp.take_along_axis(shards, slots.astype(jnp.int32)[:, :, None], axis=1).reshape(CENTERS, D)
    center_unit = unit_rows(placed)
    coef_low = coefs.astype(jnp.bfloat16)

    def member(grads, inputs):
        pool_rows, label_rows, member_order = inputs
        previous_x = None
        previous_r = None
        for step in range(INNER):
            batch_ids = member_order[step * B:(step + 1) * B]
            xunit = unit_rows(jnp.take(pool_rows, batch_ids, axis=0))
            target = jnp.take(label_rows, batch_ids, axis=0).astype(jnp.float32)
            kernel_rows = kernel_block(xunit, center_unit, sharpness)
            predicted = jnp.dot(kernel_rows, coef_low, preferred_element_type=jnp.float32) * inv_root
            if step > 0:
                local_kern = kernel_block(xunit, previous_x, sharpness)
                predicted = predicted - 2.0 / B * jnp.dot(local_kern, previous_r, preferred_element_type=jnp.float32)
            resid = (predicted - target).astype(jnp.bfloat16)
            grads = grads + lax.dot_general(kernel_rows, resid, (((0,), (0,)), ((), ())), preferred_element_type=jnp.float32)
            previous_x = xunit
            previous_r = resid
        return (grads, previous_r)
    grads, last_residual = lax.scan(member, jnp.zeros((CENTERS, C), jnp.float32), (pool, labels, order))
    new_coefs = coefs - 0.5 * inv_root * grads
    return (new_coefs, last_residual)
```

```python
import functools
import math

import jax
import jax.numpy as jnp
from jax import lax
from jax.experimental import pallas as pl
from jax.experimental.pallas import tpu as pltpu
from jax.sharding import PartitionSpec as P

INNER = 2
WIDTH = 256
F32 = jnp.float32
BF16 = jnp.bfloat16
MESH = pl.DeviceIdType.MESH


def one_hot(column, count):
    lane = lax.broadcasted_iota(jnp.int32, column.shape, 1)
    pieces = [
        jnp.where(column == lane + 128 * g, 1.0, 0.0).astype(BF16) for g in range(count // 128)
    ]
    return jnp.concatenate(pieces, axis=1)


def unit_rows(widened):
    scale = lax.rsqrt(jnp.sum(widened * widened, axis=-1, keepdims=True) + 1e-06)
    return (widened * scale).astype(BF16)


def kernel_block(left, right, sharpness):
    cosine = lax.dot_general(left, right, (((1,), (1,)), ((), ())), preferred_element_type=F32)
    distance = jnp.sqrt(2.0 - 2.0 * cosine + 0.01)
    return jnp.exp((math.sqrt(2.01) - distance) * sharpness).astype(BF16)


def column_of(row):
    return jnp.broadcast_to(row, (128, row.shape[1])).T


def body(
    nw, nz, nc, cen_h, coef_h, slots_h, pool_h, lab_h, order_h, new_ref, last_ref,
    cen, coef, slots, pool, lab, order, slotc, ordc, xu, cu, kx, kt, lk, tgt,
    cbuf, part, prec, xs, xr, rbuf, grad, gs, gr,
    lsem, ag_s, ag_r, pp_s, pp_r, xx_s, xx_r, rr_s, rr_r, rs_s, rs_r,
):
    nx = nw // 2
    batch, centers_n, width = kx.shape[0] // INNER, kx.shape[1], cen.shape[1]
    pool_n, outs = lab.shape[1], coef.shape[1]
    rows, share = coef.shape[0], batch // nw
    half = batch // 2
    sharpness = math.sqrt(width) / 1.5
    inv_root = 1.0 / math.sqrt(centers_n * nw)
    z = lax.axis_index("narrow")
    w = lax.axis_index("wide")
    c, x = lax.rem(w, 2), lax.div(w, 2)
    mate = w + 1 - 2 * c
    spans = [min(WIDTH, outs - j * WIDTH) for j in range(nc)]

    loads = [
        pltpu.make_async_copy(src, dst, lsem.at[i])
        for i, (src, dst) in enumerate(
            [(coef_h, coef), (order_h, order), (pool_h, pool), (slots_h, slots), (cen_h, cen), (lab_h, lab)]
        )
    ]
    for load in loads:
        load.start()

    barrier = pltpu.get_barrier_semaphore()

    def greet(device):
        pl.semaphore_signal(barrier, inc=1, device_id=device, device_id_type=MESH)

    for e in range(1, nw):
        greet({"wide": lax.rem(w + e, nw)})
    pl.when(z > 0)(lambda: greet({"narrow": z - 1}))
    pl.when(z < nz - 1)(lambda: greet({"narrow": z + 1}))

    loads[0].wait()
    for j in range(nc):
        value = coef[:, j * WIDTH : j * WIDTH + spans[j]].astype(BF16)
        if spans[j] < WIDTH:
            cbuf[j, z] = jnp.zeros((rows, WIDTH), BF16)
        cbuf[j, z, :, : spans[j]] = value

    inner = jnp.logical_and(z > 0, z < nz - 1)
    pl.when(inner)(lambda: pl.semaphore_wait(barrier, nw + 1))
    pl.when(jnp.logical_not(inner))(lambda: pl.semaphore_wait(barrier, nw))

    def remote(src, dst, send, recv, device):
        return pltpu.make_async_remote_copy(
            src_ref=src, dst_ref=dst, send_sem=send, recv_sem=recv, device_id=device, device_id_type=MESH
        )

    drains = []

    def gather_copy(j, side, t, shard, to):
        return remote(
            cbuf.at[j, shard], cbuf.at[j, shard], ag_s.at[j, side, t], ag_r.at[j, side, t], {"narrow": to}
        )

    def gather_arrive(j, t):
        @pl.when(z - 1 - t >= 0)
        def _():
            gather_copy(j, 0, t, z - 1 - t, z - 1).wait_recv()

        @pl.when(z + 1 + t <= nz - 1)
        def _():
            gather_copy(j, 1, t, z + 1 + t, z + 1).wait_recv()

    def gather(j, t):
        if t > 0:
            gather_arrive(j, t - 1)
        up = jnp.logical_and(z - t >= 0, z < nz - 1)
        down = jnp.logical_and(z + t <= nz - 1, z > 0)
        pl.when(up)(lambda: gather_copy(j, 0, t, z - t, z + 1).start())
        pl.when(down)(lambda: gather_copy(j, 1, t, z + t, z - 1).start())
        drains.append((up, lambda: gather_copy(j, 0, t, z - t, z + 1).wait_send()))
        drains.append((down, lambda: gather_copy(j, 1, t, z + t, z - 1).wait_send()))

    def indices():
        loads[1].wait()
        column = column_of(order[...])
        for b in range(INNER):
            for v in range(nw):
                at = (b * nw + v) * share
                ordc[2 * b + v % 2, v // 2] = column[at : at + share]

    def sample_rows(i):
        picked = one_hot(ordc[i].reshape(half, 128), pool_n)
        found = jnp.dot(picked, pool[0], preferred_element_type=F32)
        xu[i] = unit_rows(found).reshape(nx, share, width)

    def center_rows(i):
        picked = one_hot(slotc[pl.ds(pl.multiple_of(i * 256, 256), 256)], centers_n)
        found = jnp.dot(picked, cen[...], preferred_element_type=F32)
        cu[pl.ds(pl.multiple_of(i * 256, 256), 256)] = unit_rows(found)

    def kernel_rows(i):
        block = kernel_block(xu[i].reshape(half, width), cu[...], sharpness)
        kx[pl.ds(pl.multiple_of(i * half, half), half)] = block

    def over(count, step):
        lax.fori_loop(0, count, lambda i, carry: (step(i), carry)[1], 0)

    def samples():
        indices()
        loads[2].wait()
        over(2 * INNER, sample_rows)

    def centers():
        loads[3].wait()
        slotc[...] = column_of(slots[...])
        loads[4].wait()
        over(centers_n // 256, center_rows)

    def kernels():
        over(2 * INNER, kernel_rows)

    def turned():
        kt[...] = kx[...].T

    def targets():
        loads[5].wait()
        lk[...] = kernel_block(xu[2 + c, x], xu[0:2].reshape(batch, width), sharpness)
        mine = jnp.concatenate([ordc[c, x], ordc[2 + c, x]], axis=0)
        picked = one_hot(mine, pool_n)
        for j in range(nc):
            if spans[j] < WIDTH:
                tgt[j] = jnp.zeros((INNER * share, WIDTH), F32)
            tgt[j, :, : spans[j]] = jnp.dot(
                picked, lab[0, :, j * WIDTH : j * WIDTH + spans[j]], preferred_element_type=F32
            )

    def mate_copy(j):
        return remote(part.at[j, :, 1 - c], prec.at[j], pp_s.at[j], pp_r.at[j], {"wide": mate})

    def predict(j):
        gather_arrive(j, nz - 2)
        for b in range(INNER):
            product = jnp.dot(
                kx[b * batch : (b + 1) * batch],
                cbuf[j].reshape(centers_n, WIDTH),
                preferred_element_type=F32,
            )
            part[j, b] = (product * inv_root).astype(BF16).reshape(2, nx, share, WIDTH)
        mate_copy(j).start()
        drains.append((None, lambda: mate_copy(j).wait_send()))

    def row_copy(j, d):
        to = lax.rem(x + d, nx)
        return remote(
            xs.at[j, d - 1], xr.at[j, d - 1], xx_s.at[j, d - 1], xx_r.at[j, d - 1], {"wide": 2 * to + c}
        )

    def exchange(j):
        mate_copy(j).wait_recv()
        for d in range(1, nx):
            to = lax.rem(x + d, nx)
            xs[j, d - 1] = (part[j, :, c, to].astype(F32) + prec[j, :, to].astype(F32)).astype(BF16)
            row_copy(j, d).start()
            drains.append((None, lambda d=d: row_copy(j, d).wait_send()))

    def resid_copy(j, b, e):
        block = rbuf.at[j, b, c, x]
        return remote(
            block, block, rr_s.at[j, b, e - 1], rr_r.at[j, b, e - 1], {"wide": lax.rem(w + e, nw)}
        )

    def spread(j, b):
        for e in range(1, nw):
            resid_copy(j, b, e).start()
            drains.append((None, lambda e=e: resid_copy(j, b, e).wait_send()))

    def resid_arrive(j, b):
        for e in range(1, nw):
            source = lax.rem(w + nw - e, nw)
            block = rbuf.at[j, b, lax.rem(source, 2), lax.div(source, 2)]
            remote(
                block, block, rr_s.at[j, b, e - 1], rr_r.at[j, b, e - 1], {"wide": source}
            ).wait_recv()

    def first(j):
        for d in range(1, nx):
            row_copy(j, d).wait_recv()
        total = part[j, :, c, x].astype(F32) + prec[j, :, x].astype(F32)
        for d in range(1, nx):
            total = total + xr[j, d - 1].astype(F32)
        total = total.reshape(INNER * share, WIDTH) - tgt[j]
        rbuf[j, 0, c, x] = total[:share].astype(BF16)
        spread(j, 0)
        tgt[j, share:] = total[share:]

    def second(j):
        resid_arrive(j, 0)
        bent = jnp.dot(lk[...], rbuf[j, 0].reshape(batch, WIDTH), preferred_element_type=F32)
        value = (tgt[j, share:] - 2.0 / batch * bent).astype(BF16)
        rbuf[j, 1, c, x] = value
        spread(j, 1)
        last_ref[0, :, j * WIDTH : j * WIDTH + spans[j]] = value[:, : spans[j]]

    def gradient(j):
        resid_arrive(j, 1)
        size = centers_n // 2
        for h in range(2):
            product = jnp.dot(
                kt[h * size : (h + 1) * size],
                rbuf[j].reshape(INNER * batch, WIDTH),
                preferred_element_type=F32,
            )
            grad[j, h * (nz // 2) : (h + 1) * (nz // 2)] = product.reshape(nz // 2, rows, WIDTH)

    def sum_copy(j, side, t):
        return remote(
            gs.at[j, side, t], gr.at[j, side, t], rs_s.at[j, side, t], rs_r.at[j, side, t],
            {"narrow": z + 1 - 2 * side},
        )

    def reduce_to(j, t):
        for side in range(2):
            rank = z if side == 0 else nz - 1 - z
            slot = nz - 1 - t + z if side == 0 else t - (nz - 1 - z)

            @pl.when(rank == 0)
            def _():
                gs[j, side, t] = grad[j, nz - 1 - t if side == 0 else t].astype(BF16)
                sum_copy(j, side, t).start()

            if t > 0:
                @pl.when(jnp.logical_and(rank >= 1, rank <= t))
                def _():
                    sum_copy(j, side, t - 1).wait_recv()
                    gs[j, side, t] = (grad[j, slot] + gr[j, side, t - 1].astype(F32)).astype(BF16)
                    sum_copy(j, side, t).start()

            drains.append((rank <= t, lambda side=side: sum_copy(j, side, t).wait_send()))

    def finish(j):
        for side in range(2):
            rank = z if side == 0 else nz - 1 - z

            @pl.when(rank >= 1)
            def _():
                sum_copy(j, side, nz - 2).wait_recv()
                grad[j, z] = grad[j, z] + gr[j, side, nz - 2].astype(F32)

        here = slice(j * WIDTH, j * WIDTH + spans[j])
        new_ref[:, here] = coef[:, here] - 0.5 * inv_root * grad[j, z][:, : spans[j]]

    unit = 2 * rows * WIDTH * 2 / 1e5
    steps = []
    for j in range(nc):
        begin = (nz - 1) * unit * j
        for t in range(nz - 1):
            steps.append((begin + t * (unit + 1.0), functools.partial(gather, j, t)))
        now = max(begin + (nz - 1) * (unit + 1.0), 12.0)
        for wait, step in (
            (0.0, predict), (2.0, exchange), (unit + 1.5, first), (unit + 1.5, second), (unit + 1.5, gradient),
        ):
            now += wait
            steps.append((now, functools.partial(step, j)))
        now += 0.5
        for t in range(nz - 1):
            steps.append((now, functools.partial(reduce_to, j, t)))
            now += unit + 1.5
        steps.append((now, functools.partial(finish, j)))
    for at, step in ((0.5, samples), (3.5, centers), (7.0, kernels), (10.5, targets), (11.9, turned)):
        steps.append((at, step))
    for _, step in sorted(steps, key=lambda entry: entry[0]):
        step()
    for condition, drain in drains:
        if condition is None:
            drain()
        else:
            pl.when(condition)(drain)


def local(centers, coefs, slots, pool, labels, order):
    nw, nz = lax.axis_size("wide"), lax.axis_size("narrow")
    nx = nw // 2
    cen_local, width = centers.shape
    rows, outs = coefs.shape
    nc = -(-outs // WIDTH)
    total = order.shape[1]
    batch = total // INNER
    share = batch // nw
    vmem = pltpu.VMEM
    dma = pltpu.SemaphoreType.DMA
    scratch = [
        vmem(centers.shape, BF16),
        vmem(coefs.shape, F32),
        vmem(slots.shape, jnp.int32),
        vmem(pool.shape, BF16),
        vmem(labels.shape, BF16),
        vmem(order.shape, jnp.int32),
        vmem((cen_local, 128), jnp.int32),
        vmem((2 * INNER, nx, share, 128), jnp.int32),
        vmem((2 * INNER, nx, share, width), BF16),
        vmem((cen_local, width), BF16),
        vmem((total, cen_local), BF16),
        vmem((cen_local, total), BF16),
        vmem((share, batch), BF16),
        vmem((nc, INNER * share, WIDTH), F32),
        vmem((nc, nz, rows, WIDTH), BF16),
        vmem((nc, INNER, 2, nx, share, WIDTH), BF16),
        vmem((nc, INNER, nx, share, WIDTH), BF16),
        vmem((nc, nx - 1, INNER, share, WIDTH), BF16),
        vmem((nc, nx - 1, INNER, share, WIDTH), BF16),
        vmem((nc, INNER, 2, nx, share, WIDTH), BF16),
        vmem((nc, nz, rows, WIDTH), F32),
        vmem((nc, 2, nz - 1, rows, WIDTH), BF16),
        vmem((nc, 2, nz - 1, rows, WIDTH), BF16),
        dma((6,)),
        dma((nc, 2, nz - 1)), dma((nc, 2, nz - 1)),
        dma((nc,)), dma((nc,)),
        dma((nc, nx - 1)), dma((nc, nx - 1)),
        dma((nc, INNER, nw - 1)), dma((nc, INNER, nw - 1)),
        dma((nc, 2, nz - 1)), dma((nc, 2, nz - 1)),
    ]
    anywhere = pl.BlockSpec(memory_space=pl.ANY)
    inside = pl.BlockSpec(memory_space=vmem)
    flops = 2 * total * cen_local * (width + 2 * outs)
    return pl.pallas_call(
        functools.partial(body, nw, nz, nc),
        out_shape=(
            jax.ShapeDtypeStruct((rows, outs), F32),
            jax.ShapeDtypeStruct((1, share, outs), BF16),
        ),
        in_specs=[anywhere] * 6,
        out_specs=(inside, inside),
        scratch_shapes=scratch,
        cost_estimate=pl.CostEstimate(
            flops=flops, bytes_accessed=10_000_000, transcendentals=total * cen_local
        ),
        compiler_params=pltpu.CompilerParams(
            collective_id=0, has_side_effects=True, vmem_limit_bytes=52 * 1024 * 1024
        ),
    )(centers, coefs, slots, pool, labels, order)


def solution(mesh):
    return jax.shard_map(
        local,
        mesh=mesh,
        in_specs=(
            P(("groups", "wide"), None),
            P(("groups", "wide", "narrow"), None),
            P(("groups", "wide"), None),
            P(("groups", "narrow"), None, None),
            P(("groups", "narrow"), None, None),
            P(("groups", "narrow"), None),
        ),
        out_specs=(P(("groups", "wide", "narrow"), None), P(("groups", "narrow"), "wide", None)),
        check_vma=False,
    )
```
